256 devices in a mesh: row: 8 (over y, core), col: 32 (over z, x).
Axes of the slice: x: 4, y: 4, z: 8, core: 2. Of those that a mesh axis runs over, the one named last changes fastest.
Arguments:
- prior_factors: float32 [16384, 128], P(('row', 'col')), may hold values from -6 to 6
- item_factors: bfloat16 [262144, 128], P(('row', 'col')), may hold values from -1 to 1
- user_tiles: int32 [8, 32, 40], P('row', 'col'), may hold values from 0 to 7
- item_tiles: int32 [8, 32, 40], P('row', 'col'), may hold values from 0 to 31
- tile_counts: int32 [8, 32], P('row', 'col'), may hold values from 10 to 40, as said below
- ratings: int32 [8, 32, 40, 256, 256], P('row', 'col'), may hold values from 0 to 5
Outputs:
- new_factors: float32 [16384, 128], P(('row', 'col'))
- residual: float32 [16384, 128], P(('row', 'col'))
The draws below stay inside these ranges and needn't reach their ends.
Inputs may be any that keep to these rules, and one draw needn't show every extreme that they name: `tile_counts`: some block has all 40 slots live in every draw.
All inputs are finite; a program needn't handle non-finite values.
Results may differ from the reference program's by a relative error of at most 0.012.
The reference program's roundings to bfloat16 on the way count: a program that leaves them out, or rounds other values in their place, can miss the bound.
Values may be sent and summed in bfloat16 or wider, within the bound.
No kernel may reach another device: no remote copies, remote signals or barrier semaphores. Data moves between devices by JAX's collectives and lax.ppermute only.
A program may use at most 128 MiB of HBM per device.

```python
import math
import jax
import jax.numpy as jnp
import numpy as np
from jax import lax

RANK = 128
TILE = 256
ITEM_DEV = 1024
SLOTS = 40
ITERS = 3
USERS = 16384
ITEMS = 262144
GROUP_USERS = 2048
USER_TILES = 8
ITEM_TILES = 32
N_ROW = 8
N_COL = 32


def draw_tile_counts(key, part):
    key = jax.random.fold_in(key, 11)
    first_key, second_key, third_key = jax.random.split(key, 3)
    counts = jax.random.randint(first_key, (N_ROW, N_COL), SLOTS // 4, SLOTS + 1, dtype=jnp.int32)
    row_pick = jax.random.randint(second_key, (), 0, N_ROW, dtype=jnp.int32)
    col_pick = jax.random.randint(third_key, (), 0, N_COL, dtype=jnp.int32)
    return counts.at[row_pick, col_pick].set(SLOTS)


def scaled_rows(order_key, base, power):
    shard_count = N_ROW * N_COL
    order = jax.random.permutation(order_key, shard_count)
    levels = (shard_count / (order.astype(jnp.float32) + 1.0)) ** power
    total = ITEM_DEV * jnp.sum(levels)
    row_levels = jnp.repeat(levels, ITEM_DEV, total_repeat_length=ITEMS)
    scale = jnp.sqrt(row_levels / total)
    return (base * scale[:, None]).astype(jnp.bfloat16)


def draw_item_factors(key, part):
    key = jax.random.fold_in(key, 23)
    order_key, value_key = jax.random.split(key, 2)
    base = jnp.clip(jax.random.normal(value_key, (ITEMS, RANK), jnp.float32), -4.0, 4.0)
    return scaled_rows(order_key, base, 1.5)


def set_ends(drawn, own_key, low, largest):
    extent = drawn.shape
    spot = [jax.random.randint(jax.random.fold_in(own_key, axis), (), 0, extent[axis]) for axis in range(len(extent))]
    drawn = drawn.at[tuple(spot)].set(low)
    longest = extent.index(max(extent))
    spot[longest] = (spot[longest] + 1) % extent[longest]
    return drawn.at[tuple(spot)].set(largest)


def level_of(key, extent, shards, least, top_value):
    level = 1.0
    for dim, parts in shards:
        heights = jax.random.uniform(jax.random.fold_in(jax.random.fold_in(key, 6), dim), (parts,), jnp.float32, least / len(shards), top_value / len(shards))
        level = level * jnp.repeat(jnp.exp(heights), extent[dim] // parts).reshape((-1,) + (1,) * (len(extent) - 1 - dim))
    return level


def rank_table(number_of, skew):
    loads = [(1 << 20) // math.isqrt(rank ** skew) + 1 for rank in range(1, number_of + 1)]
    width = 1 + sum(loads) // (1 << 30)
    return np.cumsum(np.array([max(1, weight // width) for weight in loads]))


def ranked_ids(rng, dims, amount, skew):
    table = rank_table(amount, skew)
    lot = jax.random.randint(jax.random.fold_in(rng, 1), dims, 0, int(table[amount - 1]))
    standing = jnp.searchsorted(jnp.asarray(table, jnp.int32), lot, side="right")
    return jax.random.permutation(jax.random.fold_in(rng, 2), amount)[standing].astype(jnp.int32)


def noise(rng, extent, width, reach, pieces=(), held_as=jnp.bfloat16):
    gain = level_of(rng, extent, pieces, -0.22, 0.18) if pieces else 1.0
    array = jax.random.normal(rng, extent, jnp.float32) * width * gain
    return jnp.minimum(jnp.maximum(array, -reach), reach).astype(held_as)


def setup_inputs(seed: int = 0) -> dict:
    key_list = jax.random.split(jax.random.key(seed), 7)
    return {
        "prior_factors": noise(key_list[0], (USERS, RANK), 1.0, 6.0, ((0, 256),), jnp.float32),
        "item_factors": draw_item_factors(jax.random.fold_in(key_list[6], 71), 0),
        "user_tiles": set_ends(ranked_ids(key_list[2], (N_ROW, N_COL, SLOTS), USER_TILES, 2), jax.random.fold_in(key_list[2], 3), 0, USER_TILES - 1).astype(jnp.int32),
        "item_tiles": set_ends(jax.random.randint(key_list[3], (N_ROW, N_COL, SLOTS), 0, ITEM_TILES), jax.random.fold_in(key_list[3], 1), 0, ITEM_TILES - 1).astype(jnp.int32),
        "tile_counts": draw_tile_counts(jax.random.fold_in(key_list[6], 71), 0),
        "ratings": set_ends(jax.random.randint(key_list[5], (N_ROW, N_COL, SLOTS, TILE, TILE), 0, 6), jax.random.fold_in(key_list[5], 1), 0, 5).astype(jnp.int32),
    }


confidence = 40.0
ridge_term = 0.1


def tile_term(rows, item_panel, users, items, count, rates, first):
    user_blocks = rows.reshape(-1, TILE, RANK)[users].astype(jnp.float32)
    item_blocks = item_panel.reshape(-1, TILE, RANK)[items].astype(jnp.float32)
    scores = jnp.einsum('tuk,tik->tui', user_blocks, item_blocks)
    rate = rates.astype(jnp.float32)
    live = (jnp.arange(SLOTS) < count)[:, None, None]
    if first:
        coef = jnp.where(rate > 0, 1.0 + confidence * rate * (1.0 - scores), 0.0)
    else:
        coef = confidence * rate * scores
    coef = jnp.where(live, coef, 0.0).astype(jnp.bfloat16)
    contrib = jnp.einsum('tui,tik->tuk', coef.astype(jnp.float32), item_blocks)
    total = jnp.zeros((rows.shape[0] // TILE, TILE, RANK), jnp.float32).at[users].add(contrib)
    return total.reshape(rows.shape[0], RANK)


def reference(prior_factors, item_factors, user_tiles, item_tiles, tile_counts, ratings):
    panels = item_factors.reshape(N_ROW, N_COL, ITEM_DEV, RANK).transpose(1, 0, 2, 3)
    panels = panels.reshape(N_COL, N_ROW * ITEM_DEV, RANK)
    gram_matrix = jnp.dot(item_factors.T, item_factors, preferred_element_type=jnp.float32)
    shifted = gram_matrix + ridge_term * jnp.eye(RANK, dtype=jnp.float32)

    def group_sum(field, first):
        groups = field.astype(jnp.bfloat16).reshape(N_ROW, GROUP_USERS, RANK)

        def one_group(inputs):
            rows, users, items, counts, rates = inputs

            def add_block(total, block):
                item_panel, block_users, block_items, count, block_rates = block
                return total + tile_term(rows, item_panel, block_users, block_items, count, block_rates, first), None

            init = jnp.zeros((GROUP_USERS, RANK), jnp.float32)
            total, unused = lax.scan(add_block, init, (panels, users, items, counts, rates))
            return total

        out = lax.map(one_group, (groups, user_tiles, item_tiles, tile_counts, ratings))
        return out.reshape(USERS, RANK)

    def apply_shift(field):
        return jnp.dot(field, shifted, precision=lax.Precision.HIGHEST)

    new_factors = prior_factors
    residual = group_sum(prior_factors, True) - apply_shift(prior_factors)
    direction = residual
    norm_now = jnp.sum(residual * residual, axis=1, keepdims=True)
    for iteration in range(ITERS):
        image = group_sum(direction, False) + apply_shift(direction)
        step_size = norm_now / jnp.sum(direction * image, axis=1, keepdims=True)
        new_factors = new_factors + step_size * direction
        residual = residual - step_size * image
        norm_next = jnp.sum(residual * residual, axis=1, keepdims=True)
        direction = residual + (norm_next / norm_now) * direction
        norm_now = norm_next
    return new_factors, residual
```

```python
import functools

import jax
import jax.numpy as jnp
from jax import lax
from jax.experimental import pallas as pl
from jax.experimental.pallas import tpu as pltpu
from jax.sharding import PartitionSpec as P

RANK = 128
TILE = 256
ITERS = 3
GRAM_PAD = 8
GRAM_PARTS = 16

confidence = 40.0
ridge_term = 0.1

bf16 = jnp.bfloat16
f32 = jnp.float32
VMEM_LIMIT = 56 * 1024 * 1024


def params():
    return pltpu.CompilerParams(vmem_limit_bytes=VMEM_LIMIT)


def rate_kernel(step_slots, count_ref, rates_ref, out_ref):
    base = pl.program_id(0) * step_slots
    for j in range(step_slots):
        weight = jnp.where(base + j < count_ref[0], confidence, 0.0)
        out_ref[j] = (rates_ref[j].astype(f32) * weight).astype(bf16)


def scale_rates(count, rates):
    slots = rates.shape[0]
    step_slots = 4
    return pl.pallas_call(
        functools.partial(rate_kernel, step_slots),
        grid_spec=pltpu.PrefetchScalarGridSpec(
            num_scalar_prefetch=1,
            grid=(slots // step_slots,),
            in_specs=[pl.BlockSpec((step_slots, TILE, TILE), lambda i, c: (i, 0, 0))],
            out_specs=pl.BlockSpec((step_slots, TILE, TILE), lambda i, c: (i, 0, 0)),
        ),
        out_shape=jax.ShapeDtypeStruct(rates.shape, bf16),
        compiler_params=params(),
        name="scale_rates",
    )(count, rates)


def split2(x):
    high = x.astype(bf16)
    return high, (x - high.astype(f32)).astype(bf16)


def tile_kernel(first, n_peer, own, users_ref, items_ref, rates_hbm, rows_ref, panel_ref, *rest):
    if first:
        gram_ref, out_ref, rates, sems = rest
    else:
        out_ref, rates, sems = rest
    chunks = sems.shape[0]
    per = rates.shape[0] // chunks
    peers = TILE // own

    def copy(k):
        part = pl.ds(k * per, per)
        return pltpu.make_async_copy(rates_hbm.at[part], rates.at[part], sems.at[k])

    for k in range(chunks):
        copy(k).start()
    if first:
        gram = gram_ref[...]
        gram_high, gram_low = split2(gram)
        for p in range(n_peer):
            high = rows_ref[p, :own]
            low = rows_ref[p, own:2 * own]
            shift = jnp.dot(high, gram_high, preferred_element_type=f32)
            shift += jnp.dot(high, gram_low, preferred_element_type=f32)
            shift += jnp.dot(low, gram_high, preferred_element_type=f32)
            out_ref[p, :own] = -shift
            out_ref[p, own:own + 4] = gram[4 * p:4 * p + 4]
            out_ref[p, own + 4:] = jnp.zeros((GRAM_PAD - 4, RANK), f32)
    else:
        out_ref[...] = jnp.zeros_like(out_ref)

    def slot(s):
        user = users_ref[s] * peers
        item = pl.multiple_of(items_ref[s] * TILE, TILE)
        block = panel_ref[pl.ds(item, TILE), :]
        field = rows_ref[pl.ds(user, peers), :own].reshape(TILE, RANK)
        scores = lax.dot_general(
            field, block, (((1,), (1,)), ((), ())), preferred_element_type=f32
        )
        rate = rates[s].astype(f32)
        if first:
            coef = jnp.where(rate > 0, 1.0 + rate * (1.0 - scores), 0.0)
        else:
            coef = rate * scores
        contrib = jnp.dot(coef.astype(bf16), block, preferred_element_type=f32)
        out_ref[pl.ds(user, peers), :own] += contrib.reshape(peers, own, RANK)

    for k in range(chunks):
        copy(k).wait()

        def pair(i, carry):
            slot(k * per + 2 * i)
            slot(k * per + 2 * i + 1)
            return carry

        lax.fori_loop(0, per // 2, pair, 0)


def tile_pass(first, users, items, rates, rows, panel, own, gram=None):
    n_peer = rows.shape[0]
    slots = rates.shape[0]
    chunks = 5
    vmem = pl.BlockSpec(memory_space=pltpu.VMEM)
    smem = pl.BlockSpec(memory_space=pltpu.SMEM)
    out_rows = own + (GRAM_PAD if first else 0)
    operands = (users, items, rates, rows, panel) + ((gram,) if first else ())
    return pl.pallas_call(
        functools.partial(tile_kernel, first, n_peer, own),
        in_specs=[smem, smem, pl.BlockSpec(memory_space=pl.ANY)] + [vmem] * (len(operands) - 3),
        out_specs=vmem,
        out_shape=jax.ShapeDtypeStruct((n_peer, out_rows, RANK), f32),
        scratch_shapes=[
            pltpu.VMEM((slots, TILE, TILE), bf16),
            pltpu.SemaphoreType.DMA((chunks,)),
        ],
        compiler_params=params(),
        name="tile_start" if first else "tile_pass",
    )(*operands)


def start_update_kernel(own, parts_ref, prior_ref, residual_ref, sent_ref):
    total = jnp.sum(parts_ref[...], axis=0)
    residual = total[:own] - ridge_term * prior_ref[...]
    residual_ref[...] = residual
    gram = total[own:]
    gram_high, rest = split2(gram)
    rest = gram - gram_high.astype(f32)
    gram_mid, gram_low = split2(rest)
    pack = jnp.concatenate(
        [gram_high.astype(f32)[:4], gram_mid.astype(f32)[:4], gram_low.astype(f32)[:4],
         jnp.zeros((4, RANK), f32)], axis=0
    ).astype(bf16)
    sent = jnp.concatenate([residual.astype(bf16), pack], axis=0)
    sent_ref[...] = jnp.broadcast_to(sent[None], sent_ref.shape)


def start_update(parts, prior):
    n_peer = parts.shape[0]
    own = prior.shape[0]
    vmem = pl.BlockSpec(memory_space=pltpu.VMEM)
    return pl.pallas_call(
        functools.partial(start_update_kernel, own),
        in_specs=[vmem] * 2,
        out_specs=[vmem] * 2,
        out_shape=[
            jax.ShapeDtypeStruct(prior.shape, f32),
            jax.ShapeDtypeStruct((n_peer, own + GRAM_PARTS, RANK), bf16),
        ],
        compiler_params=params(),
        name="start_update",
    )(parts, prior)


def update_kernel(last, parts_ref, shift_ref, factors_ref, residual_ref, direction_ref, *outs):
    direction = direction_ref[...]
    residual = residual_ref[...]
    shift = jnp.dot(
        direction, shift_ref[...], precision=lax.Precision.HIGHEST, preferred_element_type=f32
    )
    image = jnp.sum(parts_ref[...].astype(f32), axis=0) + shift
    norm_now = jnp.sum(residual * residual, axis=1, keepdims=True)
    step_size = norm_now / jnp.sum(direction * image, axis=1, keepdims=True)
    outs[0][...] = factors_ref[...] + step_size * direction
    residual = residual - step_size * image
    outs[1][...] = residual
    if not last:
        norm_next = jnp.sum(residual * residual, axis=1, keepdims=True)
        direction = residual + norm_next / norm_now * direction
        outs[2][...] = direction
        outs[3][...] = jnp.broadcast_to(direction.astype(bf16)[None], outs[3].shape)


def update(last, parts, shifted, factors, residual, direction):
    n_peer = parts.shape[0]
    own = factors.shape[0]
    vmem = pl.BlockSpec(memory_space=pltpu.VMEM)
    state = jax.ShapeDtypeStruct(factors.shape, f32)
    shapes = [state] * 2
    if not last:
        shapes += [state, jax.ShapeDtypeStruct((n_peer, own, RANK), bf16)]
    return pl.pallas_call(
        functools.partial(update_kernel, last),
        in_specs=[vmem] * 5,
        out_specs=[vmem] * len(shapes),
        out_shape=shapes,
        compiler_params=params(),
        name="update_last" if last else "update",
    )(parts, shifted, factors, residual, direction)


def exchange(blocks):
    return lax.all_to_all(blocks, "col", 0, 0, tiled=True)


def body(prior_factors, item_factors, user_tiles, item_tiles, tile_counts, ratings):
    users = user_tiles[0, 0]
    items = item_tiles[0, 0]
    own = prior_factors.shape[0]
    n_peer = lax.axis_size("col")
    panel = lax.all_gather(item_factors, "row", axis=0, tiled=True)
    rates = scale_rates(tile_counts[0], ratings[0, 0])
    high = lax.reduce_precision(prior_factors, 8, 7)
    rows = jnp.concatenate([high, prior_factors - high], axis=0).astype(bf16)
    rows = exchange(jnp.broadcast_to(rows[None], (n_peer,) + rows.shape))
    gram = lax.dot_general(
        panel, panel, (((0,), (0,)), ((), ())), preferred_element_type=f32
    )
    parts = exchange(tile_pass(True, users, items, rates, rows, panel, own, gram))
    residual, sent = start_update(parts, prior_factors)
    direction = residual
    factors = prior_factors
    rows = exchange(sent)
    parts = rows[:, own:].astype(f32)
    gram = (parts[:, :4] + parts[:, 4:8] + parts[:, 8:12]).reshape(RANK, RANK)
    shifted = gram + ridge_term * jnp.eye(RANK, dtype=f32)
    for iteration in range(ITERS):
        last = iteration == ITERS - 1
        parts = tile_pass(False, users, items, rates, rows, panel, own)
        parts = exchange(parts)
        out = update(last, parts, shifted, factors, residual, direction)
        if last:
            return tuple(out)
        factors, residual, direction, sent = out
        rows = exchange(sent)


def solution(mesh):
    placed = (
        P(("row", "col"), None),
        P(("row", "col"), None),
        P("row", "col", None),
        P("row", "col", None),
        P("row", "col"),
        P("row", "col", None, None, None),
    )
    return jax.shard_map(
        body,
        mesh=mesh,
        in_specs=placed,
        out_specs=(P(("row", "col"), None), P(("row", "col"), None)),
        check_vma=False,
    )
```

```python
import functools

import jax
import jax.numpy as jnp
from jax import lax
from jax.experimental import pallas as pl
from jax.experimental.pallas import tpu as pltpu
from jax.sharding import PartitionSpec as P

RANK = 128
TILE = 256
ITERS = 3
CODE_ROWS = 8
START_ROWS = 16
CODE_TOP = 32704.0
GRAM_PARTS = 16

confidence = 40.0
ridge_term = 0.1

bf16 = jnp.bfloat16
f32 = jnp.float32
VMEM_LIMIT = 24 * 1024 * 1024


def params():
    return pltpu.CompilerParams(vmem_limit_bytes=VMEM_LIMIT)


def rate_kernel(step_slots, count_ref, rates_ref, out_ref):
    base = pl.program_id(0) * step_slots
    for j in range(step_slots):
        weight = jnp.where(base + j < count_ref[0], confidence, 0.0)
        out_ref[j] = (rates_ref[j].astype(f32) * weight).astype(bf16)


def scale_rates(count, rates):
    slots = rates.shape[0]
    step_slots = 8
    return pl.pallas_call(
        functools.partial(rate_kernel, step_slots),
        grid_spec=pltpu.PrefetchScalarGridSpec(
            num_scalar_prefetch=1,
            grid=(slots // step_slots,),
            in_specs=[pl.BlockSpec((step_slots, TILE, TILE), lambda i, c: (i, 0, 0))],
            out_specs=pl.BlockSpec((step_slots, TILE, TILE), lambda i, c: (i, 0, 0)),
        ),
        out_shape=jax.ShapeDtypeStruct(rates.shape, bf16),
        compiler_params=params(),
        name="scale_rates",
    )(count, rates)


def split2(x):
    high = x.astype(bf16)
    return high, (x - high.astype(f32)).astype(bf16)


def power_of_two(power):
    size = jnp.abs(power).astype(jnp.int32)
    up = jnp.ones_like(power)
    down = jnp.ones_like(power)
    for bit in range(7):
        held = (size & (1 << bit)) != 0
        up = up * jnp.where(held, 2.0 ** (1 << bit), 1.0)
        down = down * jnp.where(held, 2.0 ** -(1 << bit), 1.0)
    return jnp.where(power < 0, down, up)


def bound_power(block):
    peak = jnp.max(jnp.abs(block), axis=0, keepdims=True)
    return jnp.ceil(jnp.log2(jnp.clip(peak, 1e-30, 1e36)) + 1e-3)


def whole(x):
    return jnp.round(x).astype(jnp.int32)


def tile_kernel(first, n_peer, own, pieces, users_ref, items_ref, rates_hbm, rows_ref, *rest):
    panel_hbm = rest[:pieces]
    out_ref, rates, panel, total, sems, panel_sems = rest[pieces:]
    chunks = sems.shape[0]
    per = rates.shape[0] // chunks
    peers = TILE // own
    piece_rows = panel.shape[0] // pieces

    def copy(k):
        part = pl.ds(k * per, per)
        return pltpu.make_async_copy(rates_hbm.at[part], rates.at[part], sems.at[k])

    def panel_copy(k):
        part = pl.ds(k * piece_rows, piece_rows)
        return pltpu.make_async_copy(panel_hbm[k], panel.at[part], panel_sems.at[k])

    for k in range(pieces):
        panel_copy(k).start()
    for k in range(chunks):
        copy(k).start()
    if not first:
        total[...] = jnp.zeros_like(total)
    for k in range(pieces):
        panel_copy(k).wait()
    if first:
        gram = jnp.zeros((RANK, RANK), f32)
        for k in range(pieces):
            part = panel[k * piece_rows:(k + 1) * piece_rows]
            gram += lax.dot_general(
                part, part, (((0,), (0,)), ((), ())), preferred_element_type=f32
            )
        gram_high, gram_low = split2(gram)
        for p in range(0, n_peer, peers):
            high = rows_ref[p:p + peers, :own].reshape(TILE, RANK)
            low = rows_ref[p:p + peers, own:2 * own].reshape(TILE, RANK)
            shift = jnp.dot(high, gram_high, preferred_element_type=f32)
            shift += jnp.dot(high, gram_low, preferred_element_type=f32)
            shift += jnp.dot(low, gram_high, preferred_element_type=f32)
            total[p:p + peers] = -shift.reshape(peers, own, RANK)

    def group(start):
        slots = [start + j for j in range(per)]
        users = [users_ref[s] * peers for s in slots]
        blocks = [
            panel[pl.ds(pl.multiple_of(items_ref[s] * TILE, TILE), TILE), :] for s in slots
        ]
        fields = [rows_ref[pl.ds(u, peers), :own].reshape(TILE, RANK) for u in users]
        scores = [
            lax.dot_general(
                field, block, (((1,), (1,)), ((), ())), preferred_element_type=f32
            )
            for field, block in zip(fields, blocks)
        ]
        coefs = []
        for s, score in zip(slots, scores):
            rate = rates[s].astype(f32)
            if first:
                coef = jnp.where(rate > 0, 1.0 + rate * (1.0 - score), 0.0)
            else:
                coef = rate * score
            coefs.append(coef.astype(bf16))
        contribs = [
            jnp.dot(coef, block, preferred_element_type=f32)
            for coef, block in zip(coefs, blocks)
        ]
        for user, contrib in zip(users, contribs):
            total[pl.ds(user, peers)] += contrib.reshape(peers, own, RANK)

    for k in range(chunks):
        copy(k).wait()
        group(k * per)

    lead = out_ref.shape[1] - own
    powers = jnp.concatenate([bound_power(total[p]) for p in range(n_peer)], axis=0)
    factors = power_of_two(-powers) * CODE_TOP
    if first:
        gram_powers = jnp.concatenate(
            [bound_power(gram[4 * p:4 * p + 4]) for p in range(n_peer)], axis=0
        )
        gram_factors = power_of_two(-gram_powers) * CODE_TOP
    for p in range(n_peer):
        out_ref[p, :own] = whole(total[p] * factors[p:p + 1]).astype(jnp.int16)
        lines = [powers[p:p + 1].astype(jnp.int32)]
        if first:
            scaled = gram[4 * p:4 * p + 4] * gram_factors[p:p + 1]
            gram_high = whole(scaled)
            gram_low = whole((scaled - gram_high.astype(f32)) * CODE_TOP)
            lines += [gram_powers[p:p + 1].astype(jnp.int32), gram_high, gram_low]
        filled = sum(line.shape[0] for line in lines)
        lines.append(jnp.zeros((lead - filled, RANK), jnp.int32))
        out_ref[p, own:] = jnp.concatenate(lines, axis=0).astype(jnp.int16)


def tile_pass(first, users, items, rates, rows, panel, own):
    n_peer = rows.shape[0]
    slots = rates.shape[0]
    chunks = 5
    vmem = pl.BlockSpec(memory_space=pltpu.VMEM)
    smem = pl.BlockSpec(memory_space=pltpu.SMEM)
    hbm = pl.BlockSpec(memory_space=pl.ANY)
    pieces = len(panel)
    return pl.pallas_call(
        functools.partial(tile_kernel, first, n_peer, own, pieces),
        in_specs=[smem, smem, hbm, vmem] + [hbm] * pieces,
        out_specs=vmem,
        out_shape=jax.ShapeDtypeStruct((n_peer, own + (START_ROWS if first else CODE_ROWS), RANK), jnp.int16),
        scratch_shapes=[
            pltpu.VMEM((slots, TILE, TILE), bf16),
            pltpu.VMEM((pieces * panel[0].shape[0], RANK), bf16),
            pltpu.VMEM((n_peer, own, RANK), f32),
            pltpu.SemaphoreType.DMA((chunks,)),
            pltpu.SemaphoreType.DMA((pieces,)),
        ],
        compiler_params=params(),
        name="tile_start" if first else "tile_pass",
    )(users, items, rates, rows, *panel)


def code_lines(parts_ref, own):
    return [parts_ref[p, own:].astype(f32) for p in range(parts_ref.shape[0])]


def scales(lines, row):
    powers = jnp.concatenate([line[row:row + 1] for line in lines], axis=0)
    return power_of_two(powers) * (1.0 / CODE_TOP)


def decode_sum(parts_ref, own, lines):
    scale = scales(lines, 0)
    image = jnp.zeros((own, RANK), f32)
    for p in range(parts_ref.shape[0]):
        image += parts_ref[p, :own].astype(f32) * scale[p:p + 1]
    return image


def start_update_kernel(own, parts_ref, prior_ref, residual_ref, sent_ref):
    lines = code_lines(parts_ref, own)
    residual = decode_sum(parts_ref, own, lines) - ridge_term * prior_ref[...]
    residual_ref[...] = residual
    gram = jnp.zeros((4, RANK), f32)
    scale = scales(lines, 1)
    for p, line in enumerate(lines):
        gram += (line[2:6] + line[6:10] * (1.0 / CODE_TOP)) * scale[p:p + 1]
    gram_high, rest = split2(gram)
    rest = gram - gram_high.astype(f32)
    gram_mid, gram_low = split2(rest)
    pack = jnp.concatenate(
        [gram_high.astype(f32), gram_mid.astype(f32), gram_low.astype(f32),
         jnp.zeros((4, RANK), f32)], axis=0
    ).astype(bf16)
    sent = jnp.concatenate([residual.astype(bf16), pack], axis=0)
    sent_ref[...] = jnp.broadcast_to(sent[None], sent_ref.shape)


def start_update(parts, prior):
    n_peer = parts.shape[0]
    own = prior.shape[0]
    vmem = pl.BlockSpec(memory_space=pltpu.VMEM)
    return pl.pallas_call(
        functools.partial(start_update_kernel, own),
        in_specs=[vmem] * 2,
        out_specs=[vmem] * 2,
        out_shape=[
            jax.ShapeDtypeStruct(prior.shape, f32),
            jax.ShapeDtypeStruct((n_peer, own + GRAM_PARTS, RANK), bf16),
        ],
        compiler_params=params(),
        name="start_update",
    )(parts, prior)


def update_kernel(last, parts_ref, shift_ref, factors_ref, residual_ref, direction_ref, *outs):
    direction = direction_ref[...]
    residual = residual_ref[...]
    shift = jnp.dot(
        direction, shift_ref[...], precision=lax.Precision.HIGHEST, preferred_element_type=f32
    )
    own = direction.shape[0]
    image = decode_sum(parts_ref, own, code_lines(parts_ref, own)) + shift
    norm_now = jnp.sum(residual * residual, axis=1, keepdims=True)
    step_size = norm_now / jnp.sum(direction * image, axis=1, keepdims=True)
    outs[0][...] = factors_ref[...] + step_size * direction
    residual = residual - step_size * image
    outs[1][...] = residual
    if not last:
        norm_next = jnp.sum(residual * residual, axis=1, keepdims=True)
        direction = residual + norm_next / norm_now * direction
        outs[2][...] = direction
        outs[3][...] = jnp.broadcast_to(direction.astype(bf16)[None], outs[3].shape)


def update(last, parts, shifted, factors, residual, direction):
    n_peer = parts.shape[0]
    own = factors.shape[0]
    vmem = pl.BlockSpec(memory_space=pltpu.VMEM)
    state = jax.ShapeDtypeStruct(factors.shape, f32)
    shapes = [state] * 2
    if not last:
        shapes += [state, jax.ShapeDtypeStruct((n_peer, own, RANK), bf16)]
    return pl.pallas_call(
        functools.partial(update_kernel, last),
        in_specs=[vmem] * 5,
        out_specs=[vmem] * len(shapes),
        out_shape=shapes,
        compiler_params=params(),
        name="update_last" if last else "update",
    )(parts, shifted, factors, residual, direction)


def exchange(blocks):
    return lax.all_to_all(blocks, "col", 0, 0, tiled=True)


def gather_panel(shard, items, beside):
    n_row = lax.axis_size("row")
    me = lax.axis_index("row")
    pair = [(r, r ^ 1) for r in range(n_row)]
    mine = [shard]
    for k in range(1, n_row // 2):
        ring = [(r, (r + 2 * k) % n_row) for r in range(n_row)]
        mine.append(lax.ppermute(shard, "row", ring))
    mine, beside = lax.optimization_barrier((mine, beside))
    pieces = []
    for piece in mine:
        pieces += [piece, lax.ppermute(piece, "row", pair)]
    tiles = shard.shape[0] // TILE
    owner = items // tiles
    turn = (me // 2 - owner // 2) % (n_row // 2)
    place = turn * 2 + (owner % 2 != me % 2).astype(items.dtype)
    return pieces, place * tiles + items % tiles, beside


def body(prior_factors, item_factors, user_tiles, item_tiles, tile_counts, ratings):
    users = user_tiles[0, 0]
    items = item_tiles[0, 0]
    own = prior_factors.shape[0]
    n_peer = lax.axis_size("col")
    rates = scale_rates(tile_counts[0], ratings[0, 0])
    panel, items, rates = gather_panel(item_factors, items, rates)
    high = lax.reduce_precision(prior_factors, 8, 7)
    rows = jnp.concatenate([high, prior_factors - high], axis=0).astype(bf16)
    rows = exchange(jnp.broadcast_to(rows[None], (n_peer,) + rows.shape))
    parts = exchange(tile_pass(True, users, items, rates, rows, panel, own))
    residual, sent = start_update(parts, prior_factors)
    direction = residual
    factors = prior_factors
    rows = exchange(sent)
    parts = rows[:, own:].astype(f32)
    gram = (parts[:, :4] + parts[:, 4:8] + parts[:, 8:12]).reshape(RANK, RANK)
    shifted = gram + ridge_term * jnp.eye(RANK, dtype=f32)
    for iteration in range(ITERS):
        last = iteration == ITERS - 1
        parts = tile_pass(False, users, items, rates, rows, panel, own)
        parts = exchange(parts)
        out = update(last, parts, shifted, factors, residual, direction)
        if last:
            return tuple(out)
        factors, residual, direction, sent = out
        rows = exchange(sent)


def solution(mesh):
    placed = (
        P(("row", "col"), None),
        P(("row", "col"), None),
        P("row", "col", None),
        P("row", "col", None),
        P("row", "col"),
        P("row", "col", None, None, None),
    )
    return jax.shard_map(
        body,
        mesh=mesh,
        in_specs=placed,
        out_specs=(P(("row", "col"), None), P(("row", "col"), None)),
        check_vma=False,
    )
```

```python
import functools

import jax
import jax.numpy as jnp
from jax import lax
from jax.experimental import pallas as pl
from jax.experimental.pallas import tpu as pltpu
from jax.sharding import PartitionSpec as P

RANK = 128
TILE = 256
ITERS = 3
CODE_ROWS = 8
START_ROWS = 16
CODE_TOP = 32704.0
GRAM_ROWS = 16

confidence = 40.0
ridge_term = 0.1

bf16 = jnp.bfloat16
f32 = jnp.float32
VMEM_LIMIT = 24 * 1024 * 1024
START_LIMIT = 46 * 1024 * 1024


def params(limit=VMEM_LIMIT):
    return pltpu.CompilerParams(vmem_limit_bytes=limit)


def power_of_two(power):
    size = jnp.abs(power).astype(jnp.int32)
    up = jnp.ones_like(power)
    down = jnp.ones_like(power)
    for bit in range(7):
        held = (size & (1 << bit)) != 0
        up = up * jnp.where(held, 2.0 ** (1 << bit), 1.0)
        down = down * jnp.where(held, 2.0 ** -(1 << bit), 1.0)
    return jnp.where(power < 0, down, up)


def bound_power(block):
    peak = jnp.max(jnp.abs(block), axis=0, keepdims=True)
    return jnp.ceil(jnp.log2(jnp.clip(peak, 1e-30, 1e36)) + 1e-3)


def whole(x):
    return jnp.round(x).astype(jnp.int32)


def tile_kernel(first, n_peer, own, pieces, users_ref, items_ref, rates, rows_ref, *rest):
    if first:
        count_ref, gram_ref = rest[:2]
        panel_hbm = rest[2:2 + pieces]
        out_ref, panel, scaled_rates, total, panel_sems, ratings, rate_sems = rest[2 + pieces:]
        rates_hbm, rates = rates, ratings
    else:
        panel, out_ref, total = rest
    per = 8
    peers = TILE // own

    def panel_copy(k):
        part = pl.ds(k * (panel.shape[0] // pieces), panel.shape[0] // pieces)
        return pltpu.make_async_copy(panel_hbm[k], panel.at[part], panel_sems.at[k])

    def rate_copy(k):
        part = pl.ds(k * per, per)
        return pltpu.make_async_copy(rates_hbm.at[part], rates.at[part], rate_sems.at[k])

    if first:
        for k in range(pieces):
            panel_copy(k).start()
        for k in range(rates.shape[0] // per):
            rate_copy(k).start()
    total[...] = jnp.zeros_like(total)
    if first:
        for k in range(pieces):
            panel_copy(k).wait()

    def group(start):
        slots = [start + j for j in range(per)]
        users = [users_ref[s] * peers for s in slots]
        blocks = [
            panel[pl.ds(pl.multiple_of(items_ref[s] * TILE, TILE), TILE), :] for s in slots
        ]
        fields = [rows_ref[pl.ds(u, peers), :own].reshape(TILE, RANK) for u in users]
        scores = [
            lax.dot_general(
                field, block, (((1,), (1,)), ((), ())), preferred_element_type=f32
            )
            for field, block in zip(fields, blocks)
        ]
        coefs = []
        for s, score in zip(slots, scores):
            rate = rates[s].astype(f32)
            if first:
                rate = rate * jnp.where(s < count_ref[0], confidence, 0.0)
                scaled_rates[s] = rate.astype(bf16)
                coef = jnp.where(rate > 0, 1.0 + rate * (1.0 - score), 0.0)
            else:
                coef = rate * score
            coefs.append(coef.astype(bf16))
        contribs = [
            jnp.dot(coef, block, preferred_element_type=f32)
            for coef, block in zip(coefs, blocks)
        ]
        for user, contrib in zip(users, contribs):
            total[pl.ds(user, peers)] += contrib.reshape(peers, own, RANK)

    for k in range(rates.shape[0] // per):
        if first:
            rate_copy(k).wait()
        group(k * per)

    lead = out_ref.shape[1] - own
    powers = jnp.concatenate([bound_power(total[p]) for p in range(n_peer)], axis=0)
    factors = power_of_two(-powers) * CODE_TOP
    extra = [jnp.zeros((lead - 1, RANK), jnp.int32)]
    if first:
        gram = gram_ref[...]
        gram_power = bound_power(gram)
        scaled = gram * (power_of_two(-gram_power) * CODE_TOP)
        gram_high = whole(scaled)
        gram_low = whole((scaled - gram_high.astype(f32)) * CODE_TOP)
        extra = [gram_power.astype(jnp.int32), gram_high, gram_low,
                 jnp.zeros((lead - 2 - 2 * gram.shape[0], RANK), jnp.int32)]
    for p in range(n_peer):
        out_ref[p, :own] = whole(total[p] * factors[p:p + 1]).astype(jnp.int16)
        lines = [powers[p:p + 1].astype(jnp.int32)] + extra
        out_ref[p, own:] = jnp.concatenate(lines, axis=0).astype(jnp.int16)


def tile_pass(first, users, items, rates, rows, panel, own, count=None, gram=None):
    n_peer = rows.shape[0]
    vmem = pl.BlockSpec(memory_space=pltpu.VMEM)
    smem = pl.BlockSpec(memory_space=pltpu.SMEM)
    hbm = pl.BlockSpec(memory_space=pl.ANY)
    code_rows = own + (START_ROWS if first else CODE_ROWS)
    out_shape = [jax.ShapeDtypeStruct((n_peer, code_rows, RANK), jnp.int16)]
    scratch = [pltpu.VMEM((n_peer, own, RANK), f32)]
    specs = [smem, smem, vmem, vmem]
    operands = [users, items, rates, rows]
    pieces = 0
    if first:
        pieces = len(panel)
        out_shape.append(jax.ShapeDtypeStruct((pieces * panel[0].shape[0], RANK), bf16))
        out_shape.append(jax.ShapeDtypeStruct(rates.shape, bf16))
        scratch.append(pltpu.SemaphoreType.DMA((pieces,)))
        scratch.append(pltpu.VMEM(rates.shape, rates.dtype))
        scratch.append(pltpu.SemaphoreType.DMA((rates.shape[0] // 8,)))
        specs[2] = hbm
        specs += [smem, vmem] + [hbm] * pieces
        operands += [count, gram] + list(panel)
    else:
        specs.append(vmem)
        operands.append(panel)
    out = pl.pallas_call(
        functools.partial(tile_kernel, first, n_peer, own, pieces),
        in_specs=specs,
        out_specs=[vmem] * len(out_shape),
        out_shape=out_shape,
        scratch_shapes=scratch,
        compiler_params=params(START_LIMIT if first else VMEM_LIMIT),
        name="tile_start" if first else "tile_pass",
    )(*operands)
    return out if first else out[0]


def code_lines(parts_ref, own):
    return [parts_ref[p, own:].astype(f32) for p in range(parts_ref.shape[0])]


def scales(lines, row):
    powers = jnp.concatenate([line[row:row + 1] for line in lines], axis=0)
    return power_of_two(powers) * (1.0 / CODE_TOP)


def decode_sum(parts_ref, own, lines):
    scale = scales(lines, 0)
    image = jnp.zeros((own, RANK), f32)
    for p in range(parts_ref.shape[0]):
        image += parts_ref[p, :own].astype(f32) * scale[p:p + 1]
    return image


def start_update_kernel(own, parts_ref, prior_ref, residual_ref, shift_ref, sent_ref):
    lines = code_lines(parts_ref, own)
    scale = scales(lines, 1)
    gram = jnp.concatenate(
        [
            (line[2:6] + line[6:10] * (1.0 / CODE_TOP)) * scale[p:p + 1]
            for p, line in enumerate(lines)
        ],
        axis=0,
    )
    row = lax.broadcasted_iota(jnp.int32, gram.shape, 0)
    column = lax.broadcasted_iota(jnp.int32, gram.shape, 1)
    shifted = gram + jnp.where(row == column, ridge_term, 0.0)
    shift_ref[...] = shifted
    shift = jnp.dot(
        prior_ref[...], shifted, precision=lax.Precision.HIGHEST, preferred_element_type=f32
    )
    residual = decode_sum(parts_ref, own, lines) - shift
    residual_ref[...] = residual
    sent_ref[...] = jnp.broadcast_to(residual.astype(bf16)[None], sent_ref.shape)


def start_update(parts, prior):
    n_peer = parts.shape[0]
    own = prior.shape[0]
    vmem = pl.BlockSpec(memory_space=pltpu.VMEM)
    return pl.pallas_call(
        functools.partial(start_update_kernel, own),
        in_specs=[vmem] * 2,
        out_specs=[vmem] * 3,
        out_shape=[
            jax.ShapeDtypeStruct(prior.shape, f32),
            jax.ShapeDtypeStruct((RANK, RANK), f32),
            jax.ShapeDtypeStruct((n_peer, own, RANK), bf16),
        ],
        compiler_params=params(),
        name="start_update",
    )(parts, prior)


def prepare_kernel(own, prior_ref, shard_ref, other_ref, sent_ref):
    n_peer = sent_ref.shape[0]
    gram = jnp.zeros((RANK, RANK), f32)
    for ref in (shard_ref, other_ref):
        shard = ref[...]
        gram += lax.dot_general(
            shard, shard, (((0,), (0,)), ((), ())), preferred_element_type=f32
        )
    parts = []
    rest = gram
    for _ in range(3):
        part = rest.astype(bf16).astype(f32)
        parts.append(part)
        rest = rest - part
    prior = prior_ref[...].astype(bf16)
    rows = RANK // n_peer
    filler = jnp.zeros((GRAM_ROWS - 3 * rows, RANK), f32)
    for p in range(n_peer):
        sent_ref[p, :own] = prior
        lines = [part[rows * p:rows * p + rows] for part in parts] + [filler]
        sent_ref[p, own:] = jnp.concatenate(lines, axis=0).astype(bf16)


def prepare(prior, shard, other, n_peer):
    own = prior.shape[0]
    vmem = pl.BlockSpec(memory_space=pltpu.VMEM)
    return pl.pallas_call(
        functools.partial(prepare_kernel, own),
        in_specs=[vmem] * 3,
        out_specs=vmem,
        out_shape=jax.ShapeDtypeStruct((n_peer, own + GRAM_ROWS, RANK), bf16),
        compiler_params=params(),
        name="prepare",
    )(prior, shard, other)


def update_kernel(last, parts_ref, shift_ref, factors_ref, residual_ref, direction_ref, *outs):
    direction = direction_ref[...]
    residual = residual_ref[...]
    shift = jnp.dot(
        direction, shift_ref[...], precision=lax.Precision.HIGHEST, preferred_element_type=f32
    )
    own = direction.shape[0]
    image = decode_sum(parts_ref, own, code_lines(parts_ref, own)) + shift
    norm_now = jnp.sum(residual * residual, axis=1, keepdims=True)
    step_size = norm_now / jnp.sum(direction * image, axis=1, keepdims=True)
    outs[0][...] = factors_ref[...] + step_size * direction
    residual = residual - step_size * image
    outs[1][...] = residual
    if not last:
        norm_next = jnp.sum(residual * residual, axis=1, keepdims=True)
        direction = residual + norm_next / norm_now * direction
        outs[2][...] = direction
        outs[3][...] = jnp.broadcast_to(direction.astype(bf16)[None], outs[3].shape)


def update(last, parts, shifted, factors, residual, direction):
    n_peer = parts.shape[0]
    own = factors.shape[0]
    vmem = pl.BlockSpec(memory_space=pltpu.VMEM)
    state = jax.ShapeDtypeStruct(factors.shape, f32)
    shapes = [state] * 2
    if not last:
        shapes += [state, jax.ShapeDtypeStruct((n_peer, own, RANK), bf16)]
    return pl.pallas_call(
        functools.partial(update_kernel, last),
        in_specs=[vmem] * 5,
        out_specs=[vmem] * len(shapes),
        out_shape=shapes,
        compiler_params=params(),
        name="update_last" if last else "update",
    )(parts, shifted, factors, residual, direction)


def exchange(blocks):
    return lax.all_to_all(blocks, "col", 0, 0, tiled=True)


def along_y(x):
    n_row = lax.axis_size("row")
    return [x] + [
        lax.ppermute(x, "row", [(r, (r + 2 * k) % n_row) for r in range(n_row)])
        for k in range(1, n_row // 2)
    ]


def panel_places(items, tiles):
    n_row = lax.axis_size("row")
    me = lax.axis_index("row")
    owner = items // tiles
    turn = (me // 2 - owner // 2) % (n_row // 2)
    place = turn * 2 + (owner % 2 != me % 2).astype(items.dtype)
    return place * tiles + items % tiles


def body(prior_factors, item_factors, user_tiles, item_tiles, tile_counts, ratings):
    users = user_tiles[0, 0]
    own = prior_factors.shape[0]
    n_peer = lax.axis_size("col")
    items = panel_places(item_tiles[0, 0], item_factors.shape[0] // TILE)
    swap = [(r, r ^ 1) for r in range(lax.axis_size("row"))]
    other = lax.ppermute(item_factors, "row", swap)
    mine = along_y(item_factors)
    sent = prepare(prior_factors, item_factors, other, n_peer)

    leads = lax.axis_index("row") % 2 == 0
    rows = lax.cond(leads, exchange, lambda x: x, sent)
    rows, mine = lax.optimization_barrier((rows, mine))
    panel = [mine[0], other]
    for piece in mine[1:]:
        panel += [piece, lax.ppermute(piece, "row", swap)]
    rows, panel = lax.optimization_barrier((rows, panel))
    rows = lax.cond(leads, lambda x: x, exchange, rows)
    gram = jnp.sum(rows[:, own:].astype(f32), axis=0)
    chunk = RANK // n_peer
    gram = sum(along_y(gram[:chunk] + gram[chunk:2 * chunk] + gram[2 * chunk:3 * chunk]))
    parts, panel, rates = tile_pass(
        True, users, items, ratings[0, 0], rows, panel, own, tile_counts[0], gram
    )
    residual, shifted, sent = start_update(exchange(parts), prior_factors)
    direction = residual
    factors = prior_factors
    for iteration in range(ITERS):
        last = iteration == ITERS - 1
        rows = exchange(sent)
        parts = exchange(tile_pass(False, users, items, rates, rows, panel, own))
        out = update(last, parts, shifted, factors, residual, direction)
        if last:
            return tuple(out)
        factors, residual, direction, sent = out


def solution(mesh):
    placed = (
        P(("row", "col"), None),
        P(("row", "col"), None),
        P("row", "col", None),
        P("row", "col", None),
        P("row", "col"),
        P("row", "col", None, None, None),
    )
    return jax.shard_map(
        body,
        mesh=mesh,
        in_specs=placed,
        out_specs=(P(("row", "col"), None), P(("row", "col"), None)),
        check_vma=False,
    )
```

```python
import functools

import jax
import jax.numpy as jnp
from jax import lax
from jax.experimental import pallas as pl
from jax.experimental.pallas import tpu as pltpu
from jax.sharding import PartitionSpec as P

RANK = 128
TILE = 256
ITERS = 3
CODE_ROWS = 8
START_ROWS = 16
CODE_TOP = 32704.0
GRAM_ROWS = 16

confidence = 40.0
ridge_term = 0.1

bf16 = jnp.bfloat16
f32 = jnp.float32
VMEM_LIMIT = 24 * 1024 * 1024
START_LIMIT = 40 * 1024 * 1024


def params(limit=VMEM_LIMIT):
    return pltpu.CompilerParams(vmem_limit_bytes=limit)


def power_of_two(power):
    size = jnp.abs(power).astype(jnp.int32)
    up = jnp.ones_like(power)
    down = jnp.ones_like(power)
    for bit in range(7):
        held = (size & (1 << bit)) != 0
        up = up * jnp.where(held, 2.0 ** (1 << bit), 1.0)
        down = down * jnp.where(held, 2.0 ** -(1 << bit), 1.0)
    return jnp.where(power < 0, down, up)


def bound_power(block):
    peak = jnp.max(jnp.abs(block), axis=0, keepdims=True)
    return jnp.ceil(jnp.log2(jnp.clip(peak, 1e-30, 1e36)) + 1e-3)


def whole(x):
    return jnp.round(x).astype(jnp.int32)


def tile_kernel(first, n_peer, own, pieces, users_ref, items_ref, rates, rows_ref, *rest):
    if first:
        count_ref, gram_ref = rest[:2]
        panel_hbm = rest[2:2 + pieces]
        out_ref, panel, scaled_rates, total, panel_sems, ratings, rate_sems = rest[2 + pieces:]
        rates_hbm, rates = rates, ratings
    else:
        panel, out_ref, total = rest
    per = 8
    peers = TILE // own

    def panel_copy(k):
        part = pl.ds(k * (panel.shape[0] // pieces), panel.shape[0] // pieces)
        return pltpu.make_async_copy(panel_hbm[k], panel.at[part], panel_sems.at[k])

    def rate_copy(k):
        part = pl.ds(k * per, per)
        return pltpu.make_async_copy(rates_hbm.at[part], rates.at[part], rate_sems.at[k])

    if first:
        for k in range(pieces):
            panel_copy(k).start()
        for k in range(rates.shape[0] // per):
            rate_copy(k).start()
    total[...] = jnp.zeros_like(total)
    if first:
        for k in range(pieces):
            panel_copy(k).wait()

    def group(start):
        slots = [start + j for j in range(per)]
        users = [users_ref[s] * peers for s in slots]
        blocks = [
            panel[pl.ds(pl.multiple_of(items_ref[s] * TILE, TILE), TILE), :] for s in slots
        ]
        fields = [rows_ref[pl.ds(u, peers), :own].reshape(TILE, RANK) for u in users]
        scores = [
            lax.dot_general(
                field, block, (((1,), (1,)), ((), ())), preferred_element_type=f32
            )
            for field, block in zip(fields, blocks)
        ]
        coefs = []
        for s, score in zip(slots, scores):
            rate = rates[s].astype(f32)
            if first:
                rate = rate * jnp.where(s < count_ref[0], confidence, 0.0)
                scaled_rates[s] = rate.astype(bf16)
                coef = jnp.where(rate > 0, 1.0 + rate * (1.0 - score), 0.0)
            else:
                coef = rate * score
            coefs.append(coef.astype(bf16))
        contribs = [
            jnp.dot(coef, block, preferred_element_type=f32)
            for coef, block in zip(coefs, blocks)
        ]
        for user, contrib in zip(users, contribs):
            total[pl.ds(user, peers)] += contrib.reshape(peers, own, RANK)

    for k in range(rates.shape[0] // per):
        if first:
            rate_copy(k).wait()
        group(k * per)

    lead = out_ref.shape[1] - own
    powers = jnp.concatenate([bound_power(total[p]) for p in range(n_peer)], axis=0)
    factors = power_of_two(-powers) * CODE_TOP
    extra = [jnp.zeros((lead - 1, RANK), jnp.int32)]
    if first:
        gram = gram_ref[...]
        gram_power = bound_power(gram)
        scaled = gram * (power_of_two(-gram_power) * CODE_TOP)
        gram_high = whole(scaled)
        gram_low = whole((scaled - gram_high.astype(f32)) * CODE_TOP)
        extra = [gram_power.astype(jnp.int32), gram_high, gram_low,
                 jnp.zeros((lead - 2 - 2 * gram.shape[0], RANK), jnp.int32)]
    for p in range(n_peer):
        out_ref[p, :own] = whole(total[p] * factors[p:p + 1]).astype(jnp.int16)
        lines = [powers[p:p + 1].astype(jnp.int32)] + extra
        out_ref[p, own:] = jnp.concatenate(lines, axis=0).astype(jnp.int16)


def tile_pass(first, users, items, rates, rows, panel, own, count=None, gram=None):
    n_peer = rows.shape[0]
    vmem = pl.BlockSpec(memory_space=pltpu.VMEM)
    smem = pl.BlockSpec(memory_space=pltpu.SMEM)
    hbm = pl.BlockSpec(memory_space=pl.ANY)
    code_rows = own + (START_ROWS if first else CODE_ROWS)
    out_shape = [jax.ShapeDtypeStruct((n_peer, code_rows, RANK), jnp.int16)]
    scratch = [pltpu.VMEM((n_peer, own, RANK), f32)]
    specs = [smem, smem, vmem, vmem]
    operands = [users, items, rates, rows]
    pieces = 0
    if first:
        pieces = len(panel)
        out_shape.append(jax.ShapeDtypeStruct((pieces * panel[0].shape[0], RANK), bf16))
        out_shape.append(jax.ShapeDtypeStruct(rates.shape, bf16))
        scratch.append(pltpu.SemaphoreType.DMA((pieces,)))
        scratch.append(pltpu.VMEM(rates.shape, rates.dtype))
        scratch.append(pltpu.SemaphoreType.DMA((rates.shape[0] // 8,)))
        specs[2] = hbm
        specs += [smem, vmem] + [hbm] * pieces
        operands += [count, gram] + list(panel)
    else:
        specs.append(vmem)
        operands.append(panel)
    out = pl.pallas_call(
        functools.partial(tile_kernel, first, n_peer, own, pieces),
        in_specs=specs,
        out_specs=[vmem] * len(out_shape),
        out_shape=out_shape,
        scratch_shapes=scratch,
        compiler_params=params(START_LIMIT if first else VMEM_LIMIT),
        name="tile_start" if first else "tile_pass",
    )(*operands)
    return out if first else out[0]


def code_lines(parts_ref, own):
    return [parts_ref[p, own:].astype(f32) for p in range(parts_ref.shape[0])]


def scales(lines, row):
    powers = jnp.concatenate([line[row:row + 1] for line in lines], axis=0)
    return power_of_two(powers) * (1.0 / CODE_TOP)


def decode_sum(parts_ref, own, lines):
    scale = scales(lines, 0)
    image = jnp.zeros((own, RANK), f32)
    for p in range(parts_ref.shape[0]):
        image += parts_ref[p, :own].astype(f32) * scale[p:p + 1]
    return image


def start_update_kernel(own, parts_ref, prior_ref, residual_ref, shift_ref, sent_ref):
    lines = code_lines(parts_ref, own)
    scale = scales(lines, 1)
    gram = jnp.concatenate(
        [
            (line[2:6] + line[6:10] * (1.0 / CODE_TOP)) * scale[p:p + 1]
            for p, line in enumerate(lines)
        ],
        axis=0,
    )
    row = lax.broadcasted_iota(jnp.int32, gram.shape, 0)
    column = lax.broadcasted_iota(jnp.int32, gram.shape, 1)
    shifted = gram + jnp.where(row == column, ridge_term, 0.0)
    shift_ref[...] = shifted
    shift = jnp.dot(
        prior_ref[...], shifted, precision=lax.Precision.HIGHEST, preferred_element_type=f32
    )
    residual = decode_sum(parts_ref, own, lines) - shift
    residual_ref[...] = residual
    sent_ref[...] = jnp.broadcast_to(residual.astype(bf16)[None], sent_ref.shape)


def start_update(parts, prior):
    n_peer = parts.shape[0]
    own = prior.shape[0]
    vmem = pl.BlockSpec(memory_space=pltpu.VMEM)
    return pl.pallas_call(
        functools.partial(start_update_kernel, own),
        in_specs=[vmem] * 2,
        out_specs=[vmem] * 3,
        out_shape=[
            jax.ShapeDtypeStruct(prior.shape, f32),
            jax.ShapeDtypeStruct((RANK, RANK), f32),
            jax.ShapeDtypeStruct((n_peer, own, RANK), bf16),
        ],
        compiler_params=params(),
        name="start_update",
    )(parts, prior)


def prepare_kernel(own, prior_ref, shard_ref, other_ref, sent_ref):
    n_peer = sent_ref.shape[0]
    gram = jnp.zeros((RANK, RANK), f32)
    for ref in (shard_ref, other_ref):
        shard = ref[...]
        gram += lax.dot_general(
            shard, shard, (((0,), (0,)), ((), ())), preferred_element_type=f32
        )
    parts = []
    rest = gram
    for _ in range(3):
        part = rest.astype(bf16).astype(f32)
        parts.append(part)
        rest = rest - part
    prior = prior_ref[...].astype(bf16)
    rows = RANK // n_peer
    filler = jnp.zeros((GRAM_ROWS - 3 * rows, RANK), f32)
    for p in range(n_peer):
        sent_ref[p, :own] = prior
        lines = [part[rows * p:rows * p + rows] for part in parts] + [filler]
        sent_ref[p, own:] = jnp.concatenate(lines, axis=0).astype(bf16)


def prepare(prior, shard, other, n_peer):
    own = prior.shape[0]
    vmem = pl.BlockSpec(memory_space=pltpu.VMEM)
    return pl.pallas_call(
        functools.partial(prepare_kernel, own),
        in_specs=[vmem] * 3,
        out_specs=vmem,
        out_shape=jax.ShapeDtypeStruct((n_peer, own + GRAM_ROWS, RANK), bf16),
        compiler_params=params(),
        name="prepare",
    )(prior, shard, other)


def update_kernel(last, parts_ref, shift_ref, factors_ref, residual_ref, direction_ref, *outs):
    direction = direction_ref[...]
    residual = residual_ref[...]
    shift = jnp.dot(
        direction, shift_ref[...], precision=lax.Precision.HIGHEST, preferred_element_type=f32
    )
    own = direction.shape[0]
    image = decode_sum(parts_ref, own, code_lines(parts_ref, own)) + shift
    norm_now = jnp.sum(residual * residual, axis=1, keepdims=True)
    step_size = norm_now / jnp.sum(direction * image, axis=1, keepdims=True)
    outs[0][...] = factors_ref[...] + step_size * direction
    residual = residual - step_size * image
    outs[1][...] = residual
    if not last:
        norm_next = jnp.sum(residual * residual, axis=1, keepdims=True)
        direction = residual + norm_next / norm_now * direction
        outs[2][...] = direction
        outs[3][...] = jnp.broadcast_to(direction.astype(bf16)[None], outs[3].shape)


def update(last, parts, shifted, factors, residual, direction):
    n_peer = parts.shape[0]
    own = factors.shape[0]
    vmem = pl.BlockSpec(memory_space=pltpu.VMEM)
    state = jax.ShapeDtypeStruct(factors.shape, f32)
    shapes = [state] * 2
    if not last:
        shapes += [state, jax.ShapeDtypeStruct((n_peer, own, RANK), bf16)]
    return pl.pallas_call(
        functools.partial(update_kernel, last),
        in_specs=[vmem] * 5,
        out_specs=[vmem] * len(shapes),
        out_shape=shapes,
        compiler_params=params(),
        name="update_last" if last else "update",
    )(parts, shifted, factors, residual, direction)


def exchange(blocks):
    return lax.all_to_all(blocks, "col", 0, 0, tiled=True)


def along_y(x):
    n_row = lax.axis_size("row")
    return [x] + [
        lax.ppermute(x, "row", [(r, (r + 2 * k) % n_row) for r in range(n_row)])
        for k in range(1, n_row // 2)
    ]


def panel_places(items, tiles):
    n_row = lax.axis_size("row")
    me = lax.axis_index("row")
    owner = items // tiles
    turn = (me // 2 - owner // 2) % (n_row // 2)
    place = turn * 2 + (owner % 2 != me % 2).astype(items.dtype)
    return place * tiles + items % tiles


def body(prior_factors, item_factors, user_tiles, item_tiles, tile_counts, ratings):
    users = user_tiles[0, 0]
    own = prior_factors.shape[0]
    n_peer = lax.axis_size("col")
    items = panel_places(item_tiles[0, 0], item_factors.shape[0] // TILE)
    swap = [(r, r ^ 1) for r in range(lax.axis_size("row"))]
    other = lax.ppermute(item_factors, "row", swap)
    mine = along_y(item_factors)
    sent = prepare(prior_factors, item_factors, other, n_peer)

    leads = lax.axis_index("row") % 2 == 0
    rows = lax.cond(leads, exchange, lambda x: x, sent)
    rows, mine = lax.optimization_barrier((rows, mine))
    panel = [mine[0], other]
    for piece in mine[1:]:
        panel += [piece, lax.ppermute(piece, "row", swap)]
    rows, panel = lax.optimization_barrier((rows, panel))
    rows = lax.cond(leads, lambda x: x, exchange, rows)
    gram = jnp.sum(rows[:, own:].astype(f32), axis=0)
    chunk = RANK // n_peer
    gram = sum(along_y(gram[:chunk] + gram[chunk:2 * chunk] + gram[2 * chunk:3 * chunk]))
    parts, panel, rates = tile_pass(
        True, users, items, ratings[0, 0], rows, panel, own, tile_counts[0], gram
    )
    residual, shifted, sent = start_update(exchange(parts), prior_factors)
    direction = residual
    factors = prior_factors
    for iteration in range(ITERS):
        last = iteration == ITERS - 1
        rows = exchange(sent)
        parts = exchange(tile_pass(False, users, items, rates, rows, panel, own))
        out = update(last, parts, shifted, factors, residual, direction)
        if last:
            return tuple(out)
        factors, residual, direction, sent = out


def solution(mesh):
    placed = (
        P(("row", "col"), None),
        P(("row", "col"), None),
        P("row", "col", None),
        P("row", "col", None),
        P("row", "col"),
        P("row", "col", None, None, None),
    )
    return jax.shard_map(
        body,
        mesh=mesh,
        in_specs=placed,
        out_specs=(P(("row", "col"), None), P(("row", "col"), None)),
        check_vma=False,
    )
```

```python
import functools

import jax
import jax.numpy as jnp
from jax import lax
from jax.experimental import pallas as pl
from jax.experimental.pallas import tpu as pltpu
from jax.sharding import PartitionSpec as P

RANK = 128
TILE = 256
ITERS = 3
CODE_ROWS = 8
START_ROWS = 16
CODE_TOP = 32704.0
GRAM_ROWS = 16

confidence = 40.0
ridge_term = 0.1

bf16 = jnp.bfloat16
f32 = jnp.float32
VMEM_LIMIT = 24 * 1024 * 1024
START_LIMIT = 40 * 1024 * 1024


def params(limit=VMEM_LIMIT):
    return pltpu.CompilerParams(vmem_limit_bytes=limit)


def power_of_two(power):
    size = jnp.abs(power).astype(jnp.int32)
    up = jnp.ones_like(power)
    down = jnp.ones_like(power)
    for bit in range(7):
        held = (size & (1 << bit)) != 0
        up = up * jnp.where(held, 2.0 ** (1 << bit), 1.0)
        down = down * jnp.where(held, 2.0 ** -(1 << bit), 1.0)
    return jnp.where(power < 0, down, up)


def bound_power(block):
    peak = jnp.max(jnp.abs(block), axis=0, keepdims=True)
    return jnp.ceil(jnp.log2(jnp.clip(peak, 1e-30, 1e36)) + 1e-3)


def whole(x):
    return jnp.round(x).astype(jnp.int32)


def tile_kernel(first, n_peer, own, pieces, users_ref, items_ref, rates, rows_ref, *rest):
    if first:
        count_ref = rest[0]
        panel_hbm = rest[1:1 + pieces]
        out_ref, panel, scaled_rates, total, panel_sems, ratings, rate_sems = rest[1 + pieces:]
        rates_hbm, rates = rates, ratings
    else:
        panel, out_ref, total = rest
    per = 8
    peers = TILE // own

    def panel_copy(k):
        part = pl.ds(k * (panel.shape[0] // pieces), panel.shape[0] // pieces)
        return pltpu.make_async_copy(panel_hbm[k], panel.at[part], panel_sems.at[k])

    def rate_copy(k):
        part = pl.ds(k * per, per)
        return pltpu.make_async_copy(rates_hbm.at[part], rates.at[part], rate_sems.at[k])

    if first:
        for k in range(pieces):
            panel_copy(k).start()
        for k in range(rates.shape[0] // per):
            rate_copy(k).start()
    total[...] = jnp.zeros_like(total)
    if first:
        for k in range(pieces):
            panel_copy(k).wait()

    def group(start):
        slots = [start + j for j in range(per)]
        users = [users_ref[s] * peers for s in slots]
        blocks = [
            panel[pl.ds(pl.multiple_of(items_ref[s] * TILE, TILE), TILE), :] for s in slots
        ]
        fields = [rows_ref[pl.ds(u, peers), :own].reshape(TILE, RANK) for u in users]
        scores = [
            lax.dot_general(
                field, block, (((1,), (1,)), ((), ())), preferred_element_type=f32
            )
            for field, block in zip(fields, blocks)
        ]
        coefs = []
        for s, score in zip(slots, scores):
            rate = rates[s].astype(f32)
            if first:
                rate = rate * jnp.where(s < count_ref[0], confidence, 0.0)
                scaled_rates[s] = rate.astype(bf16)
                coef = jnp.where(rate > 0, 1.0 + rate * (1.0 - score), 0.0)
            else:
                coef = rate * score
            coefs.append(coef.astype(bf16))
        contribs = [
            jnp.dot(coef, block, preferred_element_type=f32)
            for coef, block in zip(coefs, blocks)
        ]
        for user, contrib in zip(users, contribs):
            total[pl.ds(user, peers)] += contrib.reshape(peers, own, RANK)

    for k in range(rates.shape[0] // per):
        if first:
            rate_copy(k).wait()
        group(k * per)

    lead = out_ref.shape[1] - own
    powers = jnp.concatenate([bound_power(total[p]) for p in range(n_peer)], axis=0)
    factors = power_of_two(-powers) * CODE_TOP
    extra = [jnp.zeros((lead - 1, RANK), jnp.int32)]
    for p in range(n_peer):
        out_ref[p, :own] = whole(total[p] * factors[p:p + 1]).astype(jnp.int16)
        lines = [powers[p:p + 1].astype(jnp.int32)] + extra
        out_ref[p, own:] = jnp.concatenate(lines, axis=0).astype(jnp.int16)


def tile_pass(first, users, items, rates, rows, panel, own, count=None):
    n_peer = rows.shape[0]
    vmem = pl.BlockSpec(memory_space=pltpu.VMEM)
    smem = pl.BlockSpec(memory_space=pltpu.SMEM)
    hbm = pl.BlockSpec(memory_space=pl.ANY)
    code_rows = own + (START_ROWS if first else CODE_ROWS)
    out_shape = [jax.ShapeDtypeStruct((n_peer, code_rows, RANK), jnp.int16)]
    scratch = [pltpu.VMEM((n_peer, own, RANK), f32)]
    specs = [smem, smem, vmem, vmem]
    operands = [users, items, rates, rows]
    pieces = 0
    if first:
        pieces = len(panel)
        out_shape.append(jax.ShapeDtypeStruct((pieces * panel[0].shape[0], RANK), bf16))
        out_shape.append(jax.ShapeDtypeStruct(rates.shape, bf16))
        scratch.append(pltpu.SemaphoreType.DMA((pieces,)))
        scratch.append(pltpu.VMEM(rates.shape, rates.dtype))
        scratch.append(pltpu.SemaphoreType.DMA((rates.shape[0] // 8,)))
        specs[2] = hbm
        specs += [smem] + [hbm] * pieces
        operands += [count] + list(panel)
    else:
        specs.append(vmem)
        operands.append(panel)
    out = pl.pallas_call(
        functools.partial(tile_kernel, first, n_peer, own, pieces),
        in_specs=specs,
        out_specs=[vmem] * len(out_shape),
        out_shape=out_shape,
        scratch_shapes=scratch,
        compiler_params=params(START_LIMIT if first else VMEM_LIMIT),
        cost_estimate=pl.CostEstimate(
            flops=4 * rates.shape[0] * TILE * TILE * RANK,
            bytes_accessed=rates.size * rates.dtype.itemsize,
            transcendentals=0,
        ),
        name="tile_start" if first else "tile_pass",
    )(*operands)
    return out if first else out[0]


def insert_kernel(own, parts_ref, gram_ref, out_ref):
    gram = gram_ref[...]
    gram_power = bound_power(gram)
    scaled = gram * (power_of_two(-gram_power) * CODE_TOP)
    gram_high = whole(scaled)
    gram_low = whole((scaled - gram_high.astype(f32)) * CODE_TOP)
    lead = out_ref.shape[1] - own
    lines = [gram_power.astype(jnp.int32), gram_high, gram_low,
             jnp.zeros((lead - 2 - 2 * gram.shape[0], RANK), jnp.int32)]
    for p in range(out_ref.shape[0]):
        out_ref[p, :own] = parts_ref[p, :own]
        power = parts_ref[p, own:].astype(jnp.int32)[:1]
        out_ref[p, own:] = jnp.concatenate([power] + lines, axis=0).astype(jnp.int16)


def insert(parts, gram, own):
    vmem = pl.BlockSpec(memory_space=pltpu.VMEM)
    return pl.pallas_call(
        functools.partial(insert_kernel, own),
        in_specs=[vmem] * 2,
        out_specs=vmem,
        out_shape=jax.ShapeDtypeStruct(parts.shape, parts.dtype),
        compiler_params=params(),
        name="insert",
    )(parts, gram)


def code_lines(parts_ref, own):
    return [parts_ref[p, own:].astype(f32) for p in range(parts_ref.shape[0])]


def scales(lines, row):
    powers = jnp.concatenate([line[row:row + 1] for line in lines], axis=0)
    return power_of_two(powers) * (1.0 / CODE_TOP)


def decode_sum(parts_ref, own, lines):
    scale = scales(lines, 0)
    image = jnp.zeros((own, RANK), f32)
    for p in range(parts_ref.shape[0]):
        image += parts_ref[p, :own].astype(f32) * scale[p:p + 1]
    return image


def start_update_kernel(own, parts_ref, prior_ref, residual_ref, shift_ref, sent_ref):
    lines = code_lines(parts_ref, own)
    scale = scales(lines, 1)
    gram = jnp.concatenate(
        [
            (line[2:6] + line[6:10] * (1.0 / CODE_TOP)) * scale[p:p + 1]
            for p, line in enumerate(lines)
        ],
        axis=0,
    )
    row = lax.broadcasted_iota(jnp.int32, gram.shape, 0)
    column = lax.broadcasted_iota(jnp.int32, gram.shape, 1)
    shifted = gram + jnp.where(row == column, ridge_term, 0.0)
    shift_ref[...] = shifted
    shift = jnp.dot(
        prior_ref[...], shifted, precision=lax.Precision.HIGHEST, preferred_element_type=f32
    )
    residual = decode_sum(parts_ref, own, lines) - shift
    residual_ref[...] = residual
    sent_ref[...] = jnp.broadcast_to(residual.astype(bf16)[None], sent_ref.shape)


def start_update(parts, prior):
    n_peer = parts.shape[0]
    own = prior.shape[0]
    vmem = pl.BlockSpec(memory_space=pltpu.VMEM)
    return pl.pallas_call(
        functools.partial(start_update_kernel, own),
        in_specs=[vmem] * 2,
        out_specs=[vmem] * 3,
        out_shape=[
            jax.ShapeDtypeStruct(prior.shape, f32),
            jax.ShapeDtypeStruct((RANK, RANK), f32),
            jax.ShapeDtypeStruct((n_peer, own, RANK), bf16),
        ],
        compiler_params=params(),
        name="start_update",
    )(parts, prior)


def prepare_kernel(own, prior_ref, shard_ref, other_ref, sent_ref):
    n_peer = sent_ref.shape[0]
    gram = jnp.zeros((RANK, RANK), f32)
    for ref in (shard_ref, other_ref):
        shard = ref[...]
        gram += lax.dot_general(
            shard, shard, (((0,), (0,)), ((), ())), preferred_element_type=f32
        )
    parts = []
    rest = gram
    for _ in range(3):
        part = rest.astype(bf16).astype(f32)
        parts.append(part)
        rest = rest - part
    prior = prior_ref[...].astype(bf16)
    rows = RANK // n_peer
    filler = jnp.zeros((GRAM_ROWS - 3 * rows, RANK), f32)
    for p in range(n_peer):
        sent_ref[p, :own] = prior
        lines = [part[rows * p:rows * p + rows] for part in parts] + [filler]
        sent_ref[p, own:] = jnp.concatenate(lines, axis=0).astype(bf16)


def prepare(prior, shard, other, n_peer):
    own = prior.shape[0]
    vmem = pl.BlockSpec(memory_space=pltpu.VMEM)
    return pl.pallas_call(
        functools.partial(prepare_kernel, own),
        in_specs=[vmem] * 3,
        out_specs=vmem,
        out_shape=jax.ShapeDtypeStruct((n_peer, own + GRAM_ROWS, RANK), bf16),
        compiler_params=params(),
        name="prepare",
    )(prior, shard, other)


def update_kernel(last, parts_ref, shift_ref, factors_ref, residual_ref, direction_ref, *outs):
    direction = direction_ref[...]
    residual = residual_ref[...]
    shift = jnp.dot(
        direction, shift_ref[...], precision=lax.Precision.HIGHEST, preferred_element_type=f32
    )
    own = direction.shape[0]
    image = decode_sum(parts_ref, own, code_lines(parts_ref, own)) + shift
    norm_now = jnp.sum(residual * residual, axis=1, keepdims=True)
    step_size = norm_now / jnp.sum(direction * image, axis=1, keepdims=True)
    outs[0][...] = factors_ref[...] + step_size * direction
    residual = residual - step_size * image
    outs[1][...] = residual
    if not last:
        norm_next = jnp.sum(residual * residual, axis=1, keepdims=True)
        direction = residual + norm_next / norm_now * direction
        outs[2][...] = direction
        outs[3][...] = jnp.broadcast_to(direction.astype(bf16)[None], outs[3].shape)


def update(last, parts, shifted, factors, residual, direction):
    n_peer = parts.shape[0]
    own = factors.shape[0]
    vmem = pl.BlockSpec(memory_space=pltpu.VMEM)
    state = jax.ShapeDtypeStruct(factors.shape, f32)
    shapes = [state] * 2
    if not last:
        shapes += [state, jax.ShapeDtypeStruct((n_peer, own, RANK), bf16)]
    return pl.pallas_call(
        functools.partial(update_kernel, last),
        in_specs=[vmem] * 5,
        out_specs=[vmem] * len(shapes),
        out_shape=shapes,
        compiler_params=params(),
        name="update_last" if last else "update",
    )(parts, shifted, factors, residual, direction)


def exchange(blocks):
    return lax.all_to_all(blocks, "col", 0, 0, tiled=True)


def along_y(x):
    n_row = lax.axis_size("row")
    return [x] + [
        lax.ppermute(x, "row", [(r, (r + 2 * k) % n_row) for r in range(n_row)])
        for k in range(1, n_row // 2)
    ]


def panel_places(items, tiles):
    n_row = lax.axis_size("row")
    me = lax.axis_index("row")
    owner = items // tiles
    turn = (me // 2 - owner // 2) % (n_row // 2)
    place = turn * 2 + (owner % 2 != me % 2).astype(items.dtype)
    return place * tiles + items % tiles


def body(prior_factors, item_factors, user_tiles, item_tiles, tile_counts, ratings):
    users = user_tiles[0, 0]
    own = prior_factors.shape[0]
    n_peer = lax.axis_size("col")
    items = panel_places(item_tiles[0, 0], item_factors.shape[0] // TILE)
    swap = [(r, r ^ 1) for r in range(lax.axis_size("row"))]
    other = lax.ppermute(item_factors, "row", swap)
    mine = along_y(item_factors)
    sent = prepare(prior_factors, item_factors, other, n_peer)

    leads = lax.axis_index("row") % 2 == 0
    rows = lax.cond(leads, exchange, lambda x: x, sent)
    rows, mine = lax.optimization_barrier((rows, mine))
    panel = [mine[0], other]
    for piece in mine[1:]:
        panel += [piece, lax.ppermute(piece, "row", swap)]
    rows, panel = lax.optimization_barrier((rows, panel))
    rows = lax.cond(leads, lambda x: x, exchange, rows)
    gram = jnp.sum(rows[:, own:].astype(f32), axis=0)
    chunk = RANK // n_peer
    gram = sum(along_y(gram[:chunk] + gram[chunk:2 * chunk] + gram[2 * chunk:3 * chunk]))
    parts, panel, rates = tile_pass(
        True, users, items, ratings[0, 0], rows, panel, own, tile_counts[0]
    )
    parts = insert(parts, gram, own)
    residual, shifted, sent = start_update(exchange(parts), prior_factors)
    direction = residual
    factors = prior_factors
    for iteration in range(ITERS):
        last = iteration == ITERS - 1
        rows = exchange(sent)
        parts = exchange(tile_pass(False, users, items, rates, rows, panel, own))
        out = update(last, parts, shifted, factors, residual, direction)
        if last:
            return tuple(out)
        factors, residual, direction, sent = out


def solution(mesh):
    placed = (
        P(("row", "col"), None),
        P(("row", "col"), None),
        P("row", "col", None),
        P("row", "col", None),
        P("row", "col"),
        P("row", "col", None, None, None),
    )
    return jax.shard_map(
        body,
        mesh=mesh,
        in_specs=placed,
        out_specs=(P(("row", "col"), None), P(("row", "col"), None)),
        check_vma=False,
    )
```
